256 devices in a mesh: lon: 16 (over y_lo, x, core), lat: 8 (over z), dp: 2 (over y_hi).
Axes of the slice: x: 4, y: 4 (y_hi: 2, y_lo: 2; y = y_hi * 2 + y_lo), z: 8, core: 2. Of those that a mesh axis runs over, the one named last changes fastest.
Arguments:
- query: bfloat16 [128, 768, 512], P(('dp', 'lat'), 'lon'), parts along dimension 0, may hold values from -12 to 12
- keys: bfloat16 [128, 768, 512], P(('dp', 'lat'), 'lon'), parts along dimension 0, may hold values from -12 to 12
- values: bfloat16 [128, 768, 512], P(('dp', 'lat'), 'lon'), parts along dimension 0, may hold values from -6 to 6
- grad_out: bfloat16 [128, 768, 512], P(('dp', 'lat'), 'lon'), parts along dimension 0, may hold values from -6 to 6
- band_width: int32 [8], replicated, may hold values from 0 to 2, as said below
- cap_blocks: int32 [16], replicated, may hold values from 0 to 2, as said below
Outputs:
- attended: bfloat16 [128, 768, 512], P(('dp', 'lat'), 'lon'), parts along dimension 0
- query_grad: bfloat16 [128, 768, 512], P(('dp', 'lat'), 'lon'), parts along dimension 0
- key_grad: bfloat16 [128, 768, 512], P(('dp', 'lat'), 'lon'), parts along dimension 0
- value_grad: bfloat16 [128, 768, 512], P(('dp', 'lat'), 'lon'), parts along dimension 0
The draws below stay inside these ranges and needn't reach their ends.
There are 2 independent parts, one for each index of `dp`. The reference program is written for one: setup_inputs(seed, part) draws one part's arguments, and reference() takes and returns one part's arrays. A program takes and returns all parts, laid end to end along the dimension named above; an argument that names none is the same for every part. Nothing has to cross between parts.
Inputs may be any that keep to these rules, and one draw needn't show every extreme that they name: `band_width`: both pole bands take 2; some other band takes 0. `cap_blocks`: some sector takes 0 and some takes 2.
All inputs are finite; a program needn't handle non-finite values.
Results may differ from the reference program's by a relative error of at most 0.0059.
Values may be sent and summed in bfloat16 or wider, within the bound.
No kernel may reach another device: no remote copies, remote signals or barrier semaphores. Data moves between devices by JAX's collectives and lax.ppermute only.
A program may use at most 128 MiB of HBM per device.

```python
import jax
import jax.numpy as jnp
from jax import lax

HEADS = 8
HSIZE = 64
BR = 8
BC = 16
NB = 3
HALO = 2
CR = 1
HD = 512
BANDS = 8
LONS = 16
LONBLK = 48
ROWS = 64
COLS = 768
TOKB = 128
CAPK = 256


def features(key, salt):
    noise_values = jax.random.normal(jax.random.fold_in(key, salt), (ROWS, COLS, HD), jnp.float32)
    noise_values = jnp.clip(noise_values, -4.0, 4.0)
    return noise_values


def draw_query(key, part):
    result = features(key, 3)
    return result.astype(jnp.bfloat16)


def draw_keys(key, part):
    result = features(key, 4)
    return result.astype(jnp.bfloat16)


def draw_band_width(key, part):
    key = jax.random.fold_in(key, 21)
    widths = jax.random.randint(jax.random.fold_in(key, 1), (BANDS,), 0, HALO + 1)
    narrow_band = jax.random.randint(jax.random.fold_in(key, 2), (), 1, BANDS - 1)
    widths = widths.at[narrow_band].set(0).at[0].set(HALO).at[BANDS - 1].set(HALO)
    return widths.astype(jnp.int32)


def draw_cap_blocks(key, part):
    picked_blocks = jax.random.randint(jax.random.fold_in(key, 31), (LONS,), 0, NB)
    high_place = jax.random.randint(jax.random.fold_in(key, 32), (), 0, LONS)
    picked_blocks = picked_blocks.at[high_place].set(NB - 1).at[(high_place + 1) % LONS].set(0)
    return picked_blocks.astype(jnp.int32)


def level_of(own_key, dims, pieces, least, high):
    level, own = 1.0, jax.random.fold_in(own_key, 6)
    for dim, shards_of in pieces:
        heights = jnp.exp(jax.random.uniform(jax.random.fold_in(own, dim), (shards_of,), jnp.float32, least / len(pieces), high / len(pieces)))
        level = level * jnp.repeat(heights, dims[dim] // shards_of).reshape([-1 if axis == dim else 1 for axis in range(len(dims))])
    return level


def noise(key, dims, scale, reach, cuts=(), held_as=jnp.bfloat16):
    drawn = scale * jax.random.normal(key, dims, jnp.float32)
    if cuts:
        drawn = drawn * level_of(key, dims, cuts, -0.22, 0.18)
    return jnp.clip(drawn, -reach, reach).astype(held_as)


def setup_inputs(seed: int = 0, part: int = 0) -> dict:
    key_list = jax.random.split(jax.random.key(seed), 7)
    part_keys = jax.random.split(jax.random.fold_in(key_list[6], part), 7)
    return {
        "query": draw_query(jax.random.fold_in(jax.random.fold_in(key_list[6], part), 71), part),
        "keys": draw_keys(jax.random.fold_in(jax.random.fold_in(key_list[6], part), 71), part),
        "values": noise(part_keys[2], (ROWS, COLS, HD), 1.0, 6.0, ((0, 8), (1, 16))),
        "grad_out": noise(part_keys[3], (ROWS, COLS, HD), 1.0, 6.0, ((0, 8), (1, 16))),
        "band_width": draw_band_width(jax.random.fold_in(key_list[6], 71), part),
        "cap_blocks": draw_cap_blocks(jax.random.fold_in(key_list[6], 71), part),
    }


def to_blocks(grid, block_count):
    row_count = grid.shape[0]
    feature_width = grid.shape[-1]
    split_grid = grid.reshape(row_count, block_count, BC, feature_width)
    return split_grid.transpose(1, 0, 2, 3).reshape(block_count, row_count * BC, feature_width)


def from_blocks(blocks):
    block_count = blocks.shape[0]
    feature_width = blocks.shape[-1]
    split_blocks = blocks.reshape(block_count, BR, BC, feature_width)
    return split_blocks.transpose(1, 0, 2, 3).reshape(BR, block_count * BC, feature_width)


def by_heads(blocks):
    split_blocks = blocks.reshape(blocks.shape[:-1] + (HEADS, HSIZE))
    return jnp.moveaxis(split_blocks, -2, 0)


def join_heads(parts):
    moved = jnp.moveaxis(parts, 0, -2)
    return moved.reshape(moved.shape[:-2] + (HD,))


def attend(head_query_rows, windowed_key_rows, windowed_value_rows, head_output_gradient, cap_key, cap_value, permitted_mask, cap_on):
    wide = jnp.float32
    score_scale = HSIZE ** -0.5
    query_rows_flat = head_query_rows.astype(wide)
    output_gradient_rows = head_output_gradient.astype(wide)
    key_rows_flat = windowed_key_rows.astype(wide)
    value_rows_flat = windowed_value_rows.astype(wide)
    polar_key_rows = cap_key.astype(wide)
    polar_value_rows = cap_value.astype(wide)
    window_scores = jnp.where(permitted_mask, jnp.einsum('huf,hlf->hul', query_rows_flat, key_rows_flat) * score_scale, -jnp.inf)
    s_c = jnp.where(cap_on, jnp.einsum('bqe,ce->bqc', query_rows_flat, polar_key_rows) * score_scale, -jnp.inf)
    row_top = jnp.maximum(window_scores.max(-1, keepdims=True), s_c.max(-1, keepdims=True))
    e_w = jnp.exp(window_scores - row_top)
    e_c = jnp.exp(s_c - row_top)
    row_total = e_w.sum(-1, keepdims=True) + e_c.sum(-1, keepdims=True)
    p_w = e_w / row_total
    p_c = e_c / row_total
    window_probabilities = p_w.astype(jnp.bfloat16).astype(wide)
    polar_probabilities = p_c.astype(jnp.bfloat16).astype(wide)
    attended_output = jnp.einsum('ois,osg->oig', window_probabilities, value_rows_flat) + jnp.einsum('nzd,dx->nzx', polar_probabilities, polar_value_rows)
    window_prob_gradient = jnp.einsum('huf,hlf->hul', output_gradient_rows, value_rows_flat)
    dp_c = jnp.einsum('bqe,ce->bqc', output_gradient_rows, polar_value_rows)
    row_dot = (p_w * window_prob_gradient).sum(-1, keepdims=True) + (p_c * dp_c).sum(-1, keepdims=True)
    window_score_gradient = (p_w * (window_prob_gradient - row_dot)).astype(jnp.bfloat16).astype(wide)
    polar_score_gradient = (p_c * (dp_c - row_dot)).astype(jnp.bfloat16).astype(wide)
    query_gradient_term = (jnp.einsum('ois,osg->oig', window_score_gradient, key_rows_flat) + jnp.einsum('nzd,dx->nzx', polar_score_gradient, polar_key_rows)) * score_scale
    key_gradient_terms = jnp.einsum('ydw,ydt->ywt', window_score_gradient, query_rows_flat) * score_scale
    value_gradient_terms = jnp.einsum('ydw,ydt->ywt', window_probabilities, output_gradient_rows)
    cap_key_terms = jnp.einsum('bqc,bqe->ce', polar_score_gradient, query_rows_flat) * score_scale
    cap_value_terms = jnp.einsum('bqc,bqe->ce', polar_probabilities, output_gradient_rows)
    return attended_output, query_gradient_term, key_gradient_terms, value_gradient_terms, cap_key_terms, cap_value_terms


def reference(query, keys, values, grad_out, band_width, cap_blocks):
    window_span = 2 * HALO + 1

    def band_pass(band_index):
        q_grid = lax.dynamic_slice_in_dim(query, band_index * BR, BR, 0)
        k_grid = lax.dynamic_slice_in_dim(keys, band_index * BR, BR, 0)
        v_grid = lax.dynamic_slice_in_dim(values, band_index * BR, BR, 0)
        d_grid = lax.dynamic_slice_in_dim(grad_out, band_index * BR, BR, 0)
        q_blocks = to_blocks(q_grid, LONBLK)
        k_blocks = to_blocks(k_grid, LONBLK)
        v_blocks = to_blocks(v_grid, LONBLK)
        d_blocks = to_blocks(d_grid, LONBLK)
        windowed_key_rows = jnp.concatenate([jnp.roll(k_blocks, HALO - offset, axis=0) for offset in range(window_span)], axis=1)
        windowed_value_rows = jnp.concatenate([jnp.roll(v_blocks, HALO - offset, axis=0) for offset in range(window_span)], axis=1)
        first_row = jnp.where(band_index == 0, 0, BR - CR).astype(jnp.int32)
        owners = (jnp.arange(LONS, dtype=jnp.int32) * NB + cap_blocks).astype(jnp.int32)

        def cap_of(grid):
            pole_rows = lax.dynamic_slice_in_dim(grid, first_row, CR, 0).reshape(CR, LONBLK, BC, HD)
            return pole_rows[:, owners].transpose(1, 0, 2, 3).reshape(CAPK, HD)

        def add_cap(grid, cap_terms):
            pole_rows = lax.dynamic_slice_in_dim(grid, first_row, CR, 0).reshape(CR, LONBLK, BC, HD)
            placed = cap_terms.reshape(LONS, CR, BC, HD).transpose(1, 0, 2, 3)
            pole_rows = pole_rows.at[:, owners].add(placed)
            return lax.dynamic_update_slice_in_dim(grid, pole_rows.reshape(CR, COLS, HD), first_row, 0)

        offsets = jnp.arange(window_span * TOKB, dtype=jnp.int32) // TOKB
        permitted_mask = jnp.abs(offsets - HALO) <= band_width[band_index]
        cap_on = (band_index == 0) | (band_index == BANDS - 1)

        def per_head(inputs_head):
            return attend(*inputs_head, permitted_mask, cap_on)

        results = lax.map(per_head, (by_heads(q_blocks), by_heads(windowed_key_rows), by_heads(windowed_value_rows), by_heads(d_blocks), by_heads(cap_of(k_grid)), by_heads(cap_of(v_grid))))
        out_h, dq_h, dkw_h, dvw_h, dkc_h, dvc_h = results

        def fold(gradients):
            summed = jnp.zeros((LONBLK, TOKB, HD), jnp.float32)
            for offset in range(window_span):
                summed = summed + jnp.roll(gradients[:, offset * TOKB:(offset + 1) * TOKB], offset - HALO, axis=0)
            return summed

        key_total = add_cap(from_blocks(fold(join_heads(dkw_h))), join_heads(dkc_h))
        value_total = add_cap(from_blocks(fold(join_heads(dvw_h))), join_heads(dvc_h))
        return from_blocks(join_heads(out_h)), from_blocks(join_heads(dq_h)), key_total, value_total

    outputs = lax.map(band_pass, jnp.arange(BANDS, dtype=jnp.int32))
    attended, query_grad, key_grad, value_grad = outputs
    return (attended.reshape(ROWS, COLS, HD).astype(jnp.bfloat16), query_grad.reshape(ROWS, COLS, HD).astype(jnp.bfloat16), key_grad.reshape(ROWS, COLS, HD).astype(jnp.bfloat16), value_grad.reshape(ROWS, COLS, HD).astype(jnp.bfloat16))
```

```python
import functools

import jax
import jax.numpy as jnp
from jax import lax
from jax.experimental import pallas as pl
from jax.experimental.pallas import tpu as pltpu
from jax.sharding import PartitionSpec as P

HEADS = 8
HSIZE = 64
BR = 8
BC = 16
NB = 3
HALO = 2
CR = 1
BANDS = 8
HD = 512
PAIR = 2 * HSIZE
PAIRS = HD // PAIR
TOK = BR * BC
LON = 16
SPAN = 2 * HALO + 1
EXT = NB + 2 * HALO
CAPK = LON * CR * BC
CAP0 = EXT * TOK
KEYS = CAP0 + CAPK
RIM = HALO * BC
FAR = -1e30
STEPS = (8, 4, 2, 1)
VMEM = 56 * 1024 * 1024
F32 = jnp.float32
BF16 = jnp.bfloat16


def swap(value, mask):
    return lax.ppermute(value, "lon", [(i, i ^ mask) for i in range(LON)])


def shift(value, steps):
    return lax.ppermute(value, "lon", [(i, (i + steps) % LON) for i in range(LON)])


def params():
    return pltpu.CompilerParams(vmem_limit_bytes=VMEM)


def vmem(count):
    return [pl.BlockSpec(memory_space=pltpu.VMEM)] * count


def smem():
    return pl.BlockSpec(memory_space=pltpu.SMEM)


def nt(left, right):
    return lax.dot_general(left, right, (((1,), (1,)), ((), ())), preferred_element_type=F32)


def nn(left, right):
    return lax.dot_general(left, right, (((1,), (0,)), ((), ())), preferred_element_type=F32)


def pole_row(here_ref):
    return jnp.where(here_ref[0] == 0, 0, BR - CR)


def cap_column(here_ref, cap_blocks_ref):
    return pl.multiple_of(cap_blocks_ref[here_ref[1]] * BC, BC)


def edges_kernel(here_ref, cap_blocks_ref, k_ref, v_ref, east_ref, west_ref, cap_ref):
    row = pole_row(here_ref)
    column = cap_column(here_ref, cap_blocks_ref)
    for n, ref in enumerate((k_ref, v_ref)):
        cap_ref[0, n] = ref[row, pl.ds(column, BC), :]
        east_ref[n] = ref[:, NB * BC - RIM :, :]
        west_ref[n] = ref[:, :RIM, :]


def edges(here, cap_blocks, keys, values):
    rim = jax.ShapeDtypeStruct((2, BR, RIM, HD), BF16)
    return pl.pallas_call(
        edges_kernel,
        out_shape=(rim, rim, jax.ShapeDtypeStruct((1, 2, BC, HD), BF16)),
        in_specs=[smem(), smem()] + vmem(2),
        out_specs=tuple(vmem(3)),
        compiler_params=params(),
    )(here, cap_blocks, keys, values)


def block_of(ref, prefix, column, lanes):
    block = ref[prefix + (slice(None), pl.ds(column, BC), lanes)]
    return block.reshape(TOK, PAIR)


def masked_heads(block):
    lane = lax.broadcasted_iota(jnp.int32, block.shape, 1)
    zero = jnp.zeros_like(block)
    return jnp.concatenate(
        [jnp.where(lane < HSIZE, block, zero), jnp.where(lane < HSIZE, zero, block)], axis=0
    )


def attend_kernel(
    here_ref,
    width_ref,
    q_ref,
    k_ref,
    v_ref,
    d_ref,
    west_ref,
    east_ref,
    cap_ref,
    o_ref,
    dq_ref,
    own_ref,
    to_west_ref,
    to_east_ref,
    cap_keep_ref,
    cap_send_ref,
    kx,
    vx,
    kt,
    vt,
    dk,
    dv,
):
    lat = here_ref[0]
    width = width_ref[lat]
    pole = (lat == 0) | (lat == BANDS - 1)
    window_bias = [
        jnp.where(abs(offset - HALO) <= width, 0.0, FAR).astype(F32) for offset in range(SPAN)
    ]
    cap_bias = jnp.where(pole, 0.0, FAR).astype(F32)
    biases = window_bias + [cap_bias] * (CAPK // TOK)
    scale = HSIZE**-0.5

    def pair_body(pair, carry):
        lanes = pl.ds(pl.multiple_of(pair * PAIR, PAIR), PAIR)
        for n, (ref, flat, turned) in enumerate(((k_ref, kx, kt), (v_ref, vx, vt))):
            for j in range(EXT + CAPK // TOK):
                if j < HALO:
                    block = block_of(west_ref, (n,), j * BC, lanes)
                elif j < HALO + NB:
                    block = block_of(ref, (), (j - HALO) * BC, lanes)
                elif j < EXT:
                    block = block_of(east_ref, (n,), (j - HALO - NB) * BC, lanes)
                else:
                    first = (j - EXT) * (TOK // BC)
                    block = cap_ref[first : first + TOK // BC, n, :, lanes].reshape(TOK, PAIR)
                flat[j * TOK : (j + 1) * TOK, :] = block
                turned[:, j * TOK : (j + 1) * TOK] = block.T
        dk[...] = jnp.zeros_like(dk)
        dv[...] = jnp.zeros_like(dv)
        for i in range(NB):
            window = pl.ds(i * TOK, SPAN * TOK)
            cap = pl.ds(CAP0, CAPK)
            query = masked_heads(block_of(q_ref, (), i * BC, lanes) * jnp.asarray(scale, BF16))
            grad = masked_heads(block_of(d_ref, (), i * BC, lanes))
            scores = [nt(kx[part, :], query) for part in (window, cap)]
            scores = [
                part[n * TOK : (n + 1) * TOK]
                for part in scores
                for n in range(part.shape[0] // TOK)
            ]
            top = functools.reduce(
                jnp.maximum,
                [s.max(0, keepdims=True) + b for s, b in zip(scores, biases)],
            )
            weights = [jnp.exp(s - (top - b)) for s, b in zip(scores, biases)]
            total = functools.reduce(jnp.add, [w.sum(0, keepdims=True) for w in weights])
            inverse = 1.0 / total
            weights = [w * inverse for w in weights]
            grads = [nt(vx[part, :], grad) for part in (window, cap)]
            grads = [
                part[n * TOK : (n + 1) * TOK] for part in grads for n in range(part.shape[0] // TOK)
            ]
            dot = functools.reduce(
                jnp.add, [(w * g).sum(0, keepdims=True) for w, g in zip(weights, grads)]
            )
            slopes = [(w * (g - dot)).astype(BF16) for w, g in zip(weights, grads)]
            weights = [w.astype(BF16) for w in weights]
            parts = ((window, 0, SPAN), (cap, SPAN, len(weights)))
            out = jnp.zeros((PAIR, 2 * TOK), F32)
            turn = jnp.zeros((PAIR, 2 * TOK), F32)
            for part, low, high in parts:
                weight = jnp.concatenate(weights[low:high], axis=0)
                slope = jnp.concatenate(slopes[low:high], axis=0)
                out += nn(vt[:, part], weight)
                turn += nn(kt[:, part], slope)
                dv[part, :] += nn(weight, grad)
                dk[part, :] += nn(slope, query)
            for ref, value in ((o_ref, out), (dq_ref, turn * scale)):
                value = jnp.concatenate([value[:HSIZE, :TOK], value[HSIZE:, TOK:]], axis=0)
                ref[:, i * BC : (i + 1) * BC, lanes] = value.T.astype(BF16).reshape(BR, BC, PAIR)
        for n, grads in enumerate((dk, dv)):
            for j in range(EXT):
                block = grads[j * TOK : (j + 1) * TOK, :].reshape(BR, BC, PAIR)
                if j < HALO:
                    to_west_ref[n, :, j * BC : (j + 1) * BC, lanes] = block.astype(BF16)
                elif j < HALO + NB:
                    own_ref[n, :, (j - HALO) * BC : (j - HALO + 1) * BC, lanes] = block
                else:
                    column = (j - HALO - NB) * BC
                    to_east_ref[n, :, column : column + BC, lanes] = block.astype(BF16)
            half = CAPK // 2
            cap_keep_ref[:, n, :, lanes] = grads[CAP0 : CAP0 + half, :].reshape(LON // 2, BC, PAIR)
            cap_send_ref[:, n, :, lanes] = (
                grads[CAP0 + half :, :].reshape(LON // 2, BC, PAIR).astype(BF16)
            )
        return carry

    lax.fori_loop(0, PAIRS, pair_body, 0)


def attend(here, band_width, query, keys, values, grad_out, west, east, cap):
    rim = jax.ShapeDtypeStruct((2, BR, RIM, HD), BF16)
    grid = jax.ShapeDtypeStruct(query.shape, BF16)
    return pl.pallas_call(
        attend_kernel,
        out_shape=(
            grid,
            grid,
            jax.ShapeDtypeStruct((2,) + query.shape, F32),
            rim,
            rim,
            jax.ShapeDtypeStruct((LON // 2, 2, BC, HD), F32),
            jax.ShapeDtypeStruct((LON // 2, 2, BC, HD), BF16),
        ),
        in_specs=[smem(), smem()] + vmem(7),
        out_specs=tuple(vmem(7)),
        scratch_shapes=[
            pltpu.VMEM((KEYS, PAIR), BF16),
            pltpu.VMEM((KEYS, PAIR), BF16),
            pltpu.VMEM((PAIR, KEYS), BF16),
            pltpu.VMEM((PAIR, KEYS), BF16),
            pltpu.VMEM((KEYS, PAIR), F32),
            pltpu.VMEM((KEYS, PAIR), F32),
        ],
        compiler_params=params(),
    )(here, band_width, query, keys, values, grad_out, west, east, cap)


def join_kernel(
    here_ref, cap_blocks_ref, own_ref, west_ref, east_ref, keep_ref, cap_ref, dk_ref, dv_ref, total
):
    row = pole_row(here_ref)
    column = cap_column(here_ref, cap_blocks_ref)
    for n, ref in enumerate((dk_ref, dv_ref)):
        total[...] = own_ref[n]
        total[:, :RIM, :] += west_ref[n].astype(F32)
        total[:, NB * BC - RIM :, :] += east_ref[n].astype(F32)
        total[row, pl.ds(column, BC), :] += keep_ref[0, n] + cap_ref[0, n].astype(F32)
        ref[...] = total[...].astype(BF16)


def join(here, cap_blocks, own, west, east, keep, cap):
    grid = jax.ShapeDtypeStruct(own.shape[1:], BF16)
    return pl.pallas_call(
        join_kernel,
        out_shape=(grid, grid),
        in_specs=[smem(), smem()] + vmem(5),
        out_specs=tuple(vmem(2)),
        scratch_shapes=[pltpu.VMEM(own.shape[1:], F32)],
        compiler_params=params(),
    )(here, cap_blocks, own, west, east, keep, cap)


def shards(query, keys, values, grad_out, band_width, cap_blocks):
    here = jnp.stack([lax.axis_index("lat"), lax.axis_index("lon")]).astype(jnp.int32)
    to_east, to_west, cap = edges(here, cap_blocks, keys, values)
    west = shift(to_east, 1)
    east = shift(to_west, -1)
    for mask in STEPS:
        cap = jnp.concatenate([cap, swap(cap, mask)], axis=0)
    attended, query_grad, own, to_west, to_east, keep, send = attend(
        here, band_width, query, keys, values, grad_out, west, east, cap
    )
    east = shift(to_west, -1)
    west = shift(to_east, 1)
    for mask in STEPS[:0:-1]:
        total = keep + swap(send, mask).astype(F32)
        half = total.shape[0] // 2
        keep, send = total[:half], total[half:].astype(BF16)
    cap = swap(send, STEPS[0])
    key_grad, value_grad = join(here, cap_blocks, own, west, east, keep, cap)
    return attended, query_grad, key_grad, value_grad


def solution(mesh):
    grid = P(("dp", "lat"), "lon", None)
    return jax.shard_map(
        shards,
        mesh=mesh,
        in_specs=(grid, grid, grid, grid, P(), P()),
        out_specs=(grid, grid, grid, grid),
        check_vma=False,
    )
```

```python
import jax
import jax.numpy as jnp
from jax import lax
from jax.experimental import pallas as pl
from jax.experimental.pallas import tpu as pltpu
from jax.sharding import PartitionSpec as P

HSIZE = 64
BR = 8
BC = 16
NB = 3
HALO = 2
BANDS = 8
HD = 512
PAIR = 2 * HSIZE
PAIRS = HD // PAIR
TOK = BR * BC
ROWS2 = 2 * TOK
LON = 16
CAPK = LON * BC
RIM = HALO * BC
FAR = -1e30
SCALE = HSIZE**-0.5
XMASKS, YMASK, CMASK = (2, 4, 6), 8, 1
VMEM = 32 * 1024 * 1024
F32 = jnp.float32
BF16 = jnp.bfloat16
RIMS = (((0, 0, 2), (0, 1, 1)), ((0, 1, 2), (1, 0, 2)), ((1, 0, 1), (1, 1, 2)))


def swap(value, mask):
    return lax.ppermute(value, "lon", [(i, i ^ mask) for i in range(LON)])


def shift(value, steps):
    return lax.ppermute(value, "lon", [(i, (i + steps) % LON) for i in range(LON)])


def nt(left, right):
    return lax.dot_general(left, right, (((1,), (1,)), ((), ())), preferred_element_type=F32)


def nn(left, right):
    return lax.dot_general(left, right, (((1,), (0,)), ((), ())), preferred_element_type=F32)


def anywhere(count):
    return [pl.BlockSpec(memory_space=pl.ANY)] * count


def smem():
    return pl.BlockSpec(memory_space=pltpu.SMEM)


def cost(microseconds):
    return pl.CostEstimate(
        flops=0, bytes_accessed=int(microseconds * 3.5e6), transcendentals=0
    )


def lane_blocks(shape):
    return ("lanes", shape)


def stat_blocks():
    return ("lead", (PAIRS, 16, ROWS2))


def turn_blocks():
    return ("lead", (PAIRS, NB, PAIR, TOK))


STATS = jax.ShapeDtypeStruct((PAIRS, 16, ROWS2), F32)
TURNS = jax.ShapeDtypeStruct((PAIRS, NB, PAIR, TOK), F32)
GRID = (BR, NB * BC, HD)
RIM_SHAPE = (2, BR, RIM, HD)
CAP_SHAPE = (LON, 2, BC, HD)
HALF_SHAPE = (LON // 2, 2, BC, HD)


def call(kernel, us, ins, outs, out_shape, operands, part=(0, 1), into=(), behind=()):
    index, count = part
    many = isinstance(out_shape, tuple)
    kinds = list(ins) + (list(outs) if many else [outs])
    inputs = len(ins)

    def view(kind, ref, pair):
        if not isinstance(kind, tuple):
            return ref
        name, shape = kind
        if name == "lead":
            return ref.at[pl.ds(pair, 1)]
        return ref.at[(slice(None),) * (len(shape) - 1) + (pl.ds(pair * PAIR, PAIR),)]

    def whole(*refs):
        refs = refs[:inputs] + refs[inputs + len(into) + len(behind) :]
        for pair in range(PAIRS // count):
            kernel(*[view(kind, ref, pair) for kind, ref in zip(kinds, refs)])

    def spec(kind):
        if not isinstance(kind, tuple):
            return kind
        name, shape = kind
        zeros = (0,) * (len(shape) - 1)
        if name == "lead":
            return pl.BlockSpec((shape[0] // count,) + shape[1:], lambda p: (index,) + zeros)
        return pl.BlockSpec(shape[:-1] + (shape[-1] // count,), lambda p: zeros + (index,))

    specs = [spec(kind) for kind in kinds]
    return pl.pallas_call(
        whole,
        out_shape=out_shape,
        grid=(1,),
        in_specs=specs[:inputs] + anywhere(len(into) + len(behind)),
        out_specs=tuple(specs[inputs:]) if many else specs[-1],
        input_output_aliases={inputs + n: n for n in range(len(into))},
        cost_estimate=cost(us),
        compiler_params=pltpu.CompilerParams(vmem_limit_bytes=VMEM),
    )(*operands, *into, *behind)


def after(value, *others):
    return pl.pallas_call(
        lambda *refs: None,
        out_shape=jax.ShapeDtypeStruct(value.shape, value.dtype),
        in_specs=anywhere(1 + len(others)),
        out_specs=anywhere(1)[0],
        input_output_aliases={0: 0},
        cost_estimate=cost(0.1),
        compiler_params=pltpu.CompilerParams(vmem_limit_bytes=1024 * 1024),
    )(value, *others)


def held(*values):
    return pl.pallas_call(
        lambda *refs: None,
        out_shape=tuple(jax.ShapeDtypeStruct(value.shape, value.dtype) for value in values),
        in_specs=anywhere(len(values)),
        out_specs=tuple(anywhere(len(values))),
        input_output_aliases={n: n for n in range(len(values))},
        cost_estimate=cost(0.1),
        compiler_params=pltpu.CompilerParams(vmem_limit_bytes=1024 * 1024),
    )(*values)


def pole_row(lat):
    return jnp.where(lat == 0, 0, BR - 1)


def edges_kernel(cap_blocks_ref, k_ref, v_ref, cap_ref, east_ref, west_ref, sems):
    row = pole_row(lax.axis_index("lat"))
    column = pl.multiple_of(cap_blocks_ref[lax.axis_index("lon")] * BC, BC)
    copies = []
    for n, ref in enumerate((k_ref, v_ref)):
        pairs = (
            (ref.at[row, pl.ds(column, BC), :], cap_ref.at[0, n]),
            (ref.at[:, pl.ds(NB * BC - RIM, RIM), :], east_ref.at[n]),
            (ref.at[:, pl.ds(0, RIM), :], west_ref.at[n]),
        )
        for m, (source, target) in enumerate(pairs):
            copies.append(pltpu.make_async_copy(source, target, sems.at[3 * n + m]))
    for copy in copies:
        copy.start()
    for copy in copies:
        copy.wait()


def block_of(ref, prefix, column):
    return ref[prefix + (slice(None), pl.ds(column, BC), slice(None))].reshape(TOK, PAIR)


def masked_heads(block):
    lane = lax.broadcasted_iota(jnp.int32, block.shape, 1)
    zero = jnp.zeros_like(block)
    return jnp.concatenate(
        [jnp.where(lane < HSIZE, block, zero), jnp.where(lane < HSIZE, zero, block)], axis=0
    )


def query_rows(q_ref, i):
    return masked_heads(block_of(q_ref, (), i * BC) * jnp.asarray(SCALE, BF16))


def grad_rows(d_ref, i):
    return masked_heads(block_of(d_ref, (), i * BC))


def own_rows(ref):
    return jnp.concatenate([block_of(ref, (), j * BC) for j in range(NB)], axis=0)


def rim_rows(sides, n, i):
    return jnp.concatenate(
        [block_of(sides[side], (n,), block * BC) for side, block, _ in RIMS[i]], axis=0
    )


def cap_rows(cap_ref, n):
    return cap_ref[:, n].reshape(CAPK, PAIR)


def far(width, distance):
    return jnp.where(distance <= width, 0.0, FAR).astype(F32)


def cap_bias():
    lat = lax.axis_index("lat")
    return jnp.where((lat == 0) | (lat == BANDS - 1), 0.0, FAR).astype(F32)


def pieces(value):
    return [value[n * TOK : (n + 1) * TOK] for n in range(value.shape[0] // TOK)]


def column_top(scores, biases):
    tops = [s.max(0, keepdims=True) + b for s, b in zip(scores, biases)]
    top = tops[0]
    for other in tops[1:]:
        top = jnp.maximum(top, other)
    return top


def merged(scores, grads, biases, stats=None):
    top = column_top(scores, biases)
    if stats is not None:
        top = jnp.maximum(top, stats[0])
    weights = [jnp.exp(s - (top - b)) for s, b in zip(scores, biases)]
    total = sum(w.sum(0, keepdims=True) for w in weights)
    dot = sum((w * g).sum(0, keepdims=True) for w, g in zip(weights, grads))
    if stats is not None:
        fade = jnp.exp(stats[0] - top)
        total, dot = total + stats[1] * fade, dot + stats[2] * fade
    return weights, (top, total, dot)


def read_stats(ref, i):
    return tuple(ref[0, 3 * i + n : 3 * i + n + 1, :] for n in range(3))


def write_stats(ref, i, stats):
    for n, value in enumerate(stats):
        ref[0, 3 * i + n : 3 * i + n + 1, :] = value


def slopes_of(keys, values, query, grad, biases, stats):
    top, inverse, dot = stats
    weights, slopes = [], []
    for s, g, b in zip(pieces(nt(keys, query)), pieces(nt(values, grad)), biases):
        weight = jnp.exp(s - (top - b)) * inverse
        slopes.append((weight * (g - dot)).astype(BF16))
        weights.append(weight.astype(BF16))
    return jnp.concatenate(weights, axis=0), jnp.concatenate(slopes, axis=0)


def own_stats_kernel(width_ref, q_ref, k_ref, v_ref, d_ref, stats_ref):
    width = width_ref[lax.axis_index("lat")]
    keys, values = own_rows(k_ref), own_rows(v_ref)
    for i in range(NB):
        biases = [far(width, abs(j - i)) for j in range(NB)]
        scores = pieces(nt(keys, query_rows(q_ref, i)))
        grads = pieces(nt(values, grad_rows(d_ref, i)))
        write_stats(stats_ref, i, merged(scores, grads, biases)[1])


def rim_stats_kernel(width_ref, q_ref, d_ref, west_ref, east_ref, old_ref, stats_ref):
    width = width_ref[lax.axis_index("lat")]
    sides = (west_ref, east_ref)
    for i in range(NB):
        biases = [far(width, distance) for _, _, distance in RIMS[i]]
        scores = pieces(nt(rim_rows(sides, 0, i), query_rows(q_ref, i)))
        grads = pieces(nt(rim_rows(sides, 1, i), grad_rows(d_ref, i)))
        write_stats(stats_ref, i, merged(scores, grads, biases, read_stats(old_ref, i))[1])


def cap_grads_kernel(q_ref, d_ref, cap_ref, old_ref, stats_ref, keep_ref, send_ref):
    keys, values = cap_rows(cap_ref, 0), cap_rows(cap_ref, 1)
    bias = cap_bias()
    queries = [query_rows(q_ref, i) for i in range(NB)]
    outs = [grad_rows(d_ref, i) for i in range(NB)]
    weights, slopes = [], []
    for i in range(NB):
        scores, grads = nt(keys, queries[i]), nt(values, outs[i])
        (weight,), (top, total, dot) = merged([scores], [grads], [bias], read_stats(old_ref, i))
        inverse = 1.0 / total
        dot = dot * inverse
        write_stats(stats_ref, i, (top, inverse, dot))
        weight = weight * inverse
        slopes.append((weight * (grads - dot)).astype(BF16))
        weights.append(weight.astype(BF16))
    pairs = ((slopes, queries), (weights, outs))
    for n, (lefts, rights) in enumerate(pairs):
        value = nn(jnp.concatenate(lefts, axis=1), jnp.concatenate(rights, axis=0))
        value = value.reshape(LON, BC, PAIR)
        keep_ref[:, n] = value[: LON // 2]
        send_ref[:, n] = value[LON // 2 :].astype(BF16)


def heads_of(value):
    return jnp.concatenate([value[:HSIZE, :TOK], value[HSIZE:, TOK:]], axis=0)


def rim_grads_kernel(
    width_ref, q_ref, d_ref, west_ref, east_ref, stats_ref, to_west_ref, to_east_ref, ot_ref, qt_ref
):
    width = width_ref[lax.axis_index("lat")]
    sides, outs = (west_ref, east_ref), (to_west_ref, to_east_ref)
    sums = {}
    for i in range(NB):
        biases = [far(width, distance) for _, _, distance in RIMS[i]]
        query, grad = query_rows(q_ref, i), grad_rows(d_ref, i)
        keys, values = rim_rows(sides, 0, i), rim_rows(sides, 1, i)
        weights, slopes = slopes_of(keys, values, query, grad, biases, read_stats(stats_ref, i))
        ot_ref[0, i] = heads_of(nn(values.T, weights))
        qt_ref[0, i] = heads_of(nn(keys.T, slopes))
        for n, value in enumerate((nn(slopes, query), nn(weights, grad))):
            for piece, (side, block, _) in zip(pieces(value), RIMS[i]):
                key = (n, side, block)
                sums[key] = sums[key] + piece if key in sums else piece
    for (n, side, block), value in sums.items():
        outs[side][n, :, block * BC : (block + 1) * BC, :] = value.astype(BF16).reshape(
            BR, BC, PAIR
        )


def own_grads_kernel(
    width_ref,
    q_ref,
    k_ref,
    v_ref,
    d_ref,
    cap_ref,
    stats_ref,
    ot_ref,
    qt_ref,
    o_ref,
    dq_ref,
    own_ref,
):
    width = width_ref[lax.axis_index("lat")]
    bias = cap_bias()
    keys = jnp.concatenate([own_rows(k_ref), cap_rows(cap_ref, 0)], axis=0)
    values = jnp.concatenate([own_rows(v_ref), cap_rows(cap_ref, 1)], axis=0)
    keys_turned, values_turned = keys.T, values.T
    count = NB * TOK
    sums = [None, None]
    for i in range(NB):
        biases = [far(width, abs(j - i)) for j in range(NB)] + [bias] * (CAPK // TOK)
        query, grad = query_rows(q_ref, i), grad_rows(d_ref, i)
        weights, slopes = slopes_of(keys, values, query, grad, biases, read_stats(stats_ref, i))
        out = ot_ref[0, i] + heads_of(nn(values_turned, weights))
        turn = (qt_ref[0, i] + heads_of(nn(keys_turned, slopes))) * SCALE
        for ref, value in ((o_ref, out), (dq_ref, turn)):
            ref[:, i * BC : (i + 1) * BC, :] = value.T.astype(BF16).reshape(BR, BC, PAIR)
        for n, value in enumerate((nn(slopes[:count], query), nn(weights[:count], grad))):
            sums[n] = value if sums[n] is None else sums[n] + value
    for n, value in enumerate(sums):
        for j, piece in enumerate(pieces(value)):
            own_ref[n, :, j * BC : (j + 1) * BC, :] = piece.reshape(BR, BC, PAIR)


def join_kernel(
    cap_blocks_ref, own_ref, west_ref, east_ref, keep_ref, *refs
):
    row = pole_row(lax.axis_index("lat"))
    column = pl.multiple_of(cap_blocks_ref[lax.axis_index("lon")] * BC, BC)
    caps, (dk_ref, dv_ref, total) = refs[:-3], refs[-3:]
    for n, ref in enumerate((dk_ref, dv_ref)):
        total[...] = own_ref[n]
        total[:, :RIM, :] += west_ref[n].astype(F32)
        total[:, NB * BC - RIM :, :] += east_ref[n].astype(F32)
        total[row, pl.ds(column, BC), :] += keep_ref[0, n] + sum(
            ref[0, n].astype(F32) for ref in caps
        )
        ref[...] = total[...].astype(BF16)


def shards(query, keys, values, grad_out, band_width, cap_blocks):
    grid = jax.ShapeDtypeStruct(GRID, BF16)
    rim = jax.ShapeDtypeStruct(RIM_SHAPE, BF16)
    keys, values, query, grad_out = held(keys, values, query, grad_out)
    cap, to_east, to_west = pl.pallas_call(
        edges_kernel,
        out_shape=(jax.ShapeDtypeStruct((1, 2, BC, HD), BF16), rim, rim),
        in_specs=[smem()] + anywhere(2),
        out_specs=tuple(anywhere(3)),
        scratch_shapes=[pltpu.SemaphoreType.DMA((6,))],
        cost_estimate=cost(1),
        compiler_params=pltpu.CompilerParams(vmem_limit_bytes=1024 * 1024),
    )(cap_blocks, keys, values)
    west = shift(to_east, 1)
    east = shift(to_west, -1)

    g, r, w = lane_blocks(GRID), lane_blocks(RIM_SHAPE), lane_blocks((2,) + GRID)
    c, h = lane_blocks(CAP_SHAPE), lane_blocks(HALF_SHAPE)
    s, t = stat_blocks(), turn_blocks()
    received = swap(cap, YMASK)
    stats = call(
        own_stats_kernel, 0.5, [smem(), g, g, g, g], s, STATS,
        (band_width, query, keys, values, grad_out), behind=(received,),
    )
    cap = jnp.concatenate([cap, received], axis=0)
    cap = jnp.concatenate([cap] + [swap(cap, mask) for mask in XMASKS], axis=0)
    stats = call(
        rim_stats_kernel, 0.5, [smem(), g, g, r, r, s], s, STATS,
        (band_width, query, grad_out, west, east, stats),
    )
    cap = after(cap, stats)
    cap = jnp.concatenate([cap, swap(cap, CMASK)], axis=0)
    stats, keep, send = call(
        cap_grads_kernel, 3, [g, g, c, s], (s, h, h),
        (STATS, jax.ShapeDtypeStruct(HALF_SHAPE, F32), jax.ShapeDtypeStruct(HALF_SHAPE, BF16)),
        (query, grad_out, cap, stats),
    )
    total = keep + swap(send, CMASK).astype(F32)
    total = total.reshape((4, 2) + total.shape[1:])
    keep, send = total[:, 0], total[:, 1].astype(BF16)
    received = swap(send, YMASK)
    to_west, to_east, out_turned, query_turned = call(
        rim_grads_kernel, 4.5, [smem(), g, g, r, r, s], (r, r, t, t),
        (rim, rim, TURNS, TURNS),
        (band_width, query, grad_out, west, east, stats), behind=(keep,),
    )
    from_east = shift(to_west, -1)
    from_west = shift(to_east, 1)

    own_out = (grid, grid, jax.ShapeDtypeStruct((2,) + GRID, F32))
    own_in = (band_width, query, keys, values, grad_out, cap, stats, out_turned, query_turned)

    def own_part(part, into):
        kinds = [smem(), g, g, g, g, c, s, t, t]
        return call(own_grads_kernel, 4, kinds, (g, g, w), own_out, own_in, part, into, (received,))

    first = own_part((0, 2), ())
    total = keep + received.astype(F32)
    keep = total[:1]
    sends = total[1:].astype(BF16)
    caps = [swap(sends[n : n + 1], mask) for n, mask in enumerate(XMASKS)]
    attended, query_grad, own = own_part((1, 2), first)
    v = pl.BlockSpec(memory_space=pltpu.VMEM)
    key_grad, value_grad = pl.pallas_call(
        join_kernel,
        out_shape=(grid, grid),
        in_specs=[smem()] + [v] * (4 + len(caps)),
        out_specs=(v, v),
        scratch_shapes=[pltpu.VMEM(GRID, F32)],
        cost_estimate=cost(2),
        compiler_params=pltpu.CompilerParams(vmem_limit_bytes=VMEM),
    )(cap_blocks, own, from_west, from_east, keep, *caps)
    return attended, query_grad, key_grad, value_grad


def solution(mesh):
    grid = P(("dp", "lat"), "lon", None)
    return jax.shard_map(
        shards,
        mesh=mesh,
        in_specs=(grid, grid, grid, grid, P(), P()),
        out_specs=(grid, grid, grid, grid),
        check_vma=False,
    )
```

```python
import jax
import jax.numpy as jnp
from jax import lax
from jax.experimental import pallas as pl
from jax.experimental.pallas import tpu as pltpu
from jax.sharding import PartitionSpec as P

HSIZE = 64
BR = 8
BC = 16
NB = 3
HALO = 2
BANDS = 8
HD = 512
PAIR = 2 * HSIZE
PAIRS = HD // PAIR
TOK = BR * BC
ROWS2 = 2 * TOK
LON = 16
CAPK = LON * BC
RIM = HALO * BC
FAR = -1e30
SCALE = HSIZE**-0.5
XMASKS, YMASK, CMASK = (2, 4, 6), 8, 1
VMEM = 32 * 1024 * 1024
F32 = jnp.float32
BF16 = jnp.bfloat16
RIMS = (((0, 0, 2), (0, 1, 1)), ((0, 1, 2), (1, 0, 2)), ((1, 0, 1), (1, 1, 2)))


def swap(value, mask):
    return lax.ppermute(value, "lon", [(i, i ^ mask) for i in range(LON)])


def shift(value, steps):
    return lax.ppermute(value, "lon", [(i, (i + steps) % LON) for i in range(LON)])


def nt(left, right):
    return lax.dot_general(left, right, (((1,), (1,)), ((), ())), preferred_element_type=F32)


def nn(left, right):
    return lax.dot_general(left, right, (((1,), (0,)), ((), ())), preferred_element_type=F32)


def anywhere(count):
    return [pl.BlockSpec(memory_space=pl.ANY)] * count


def smem():
    return pl.BlockSpec(memory_space=pltpu.SMEM)


def cost(microseconds):
    return pl.CostEstimate(
        flops=0, bytes_accessed=int(microseconds * 3.5e6), transcendentals=0
    )


def lane_blocks(shape):
    return ("lanes", shape)


def stat_blocks():
    return ("lead", (PAIRS, 16, ROWS2))


def turn_blocks():
    return ("lead", (PAIRS, NB, PAIR, TOK))


STATS = jax.ShapeDtypeStruct((PAIRS, 16, ROWS2), F32)
TURNS = jax.ShapeDtypeStruct((PAIRS, NB, PAIR, TOK), F32)
GRID = (BR, NB * BC, HD)
RIM_SHAPE = (2, BR, RIM, HD)
CAP_SHAPE = (LON, 2, BC, HD)
HALF_SHAPE = (LON // 2, 2, BC, HD)


def call(kernel, us, ins, outs, out_shape, operands, part=(0, 1), into=(), behind=()):
    index, count = part
    many = isinstance(out_shape, tuple)
    kinds = list(ins) + (list(outs) if many else [outs])
    inputs = len(ins)

    def view(kind, ref, pair):
        if not isinstance(kind, tuple):
            return ref
        name, shape = kind
        if name == "lead":
            return ref.at[pl.ds(pair, 1)]
        return ref.at[(slice(None),) * (len(shape) - 1) + (pl.ds(pair * PAIR, PAIR),)]

    def whole(*refs):
        refs = refs[:inputs] + refs[inputs + len(into) + len(behind) :]
        for pair in range(PAIRS // count):
            kernel(*[view(kind, ref, pair) for kind, ref in zip(kinds, refs)])

    def spec(kind):
        if not isinstance(kind, tuple):
            return kind
        name, shape = kind
        zeros = (0,) * (len(shape) - 1)
        if name == "lead":
            return pl.BlockSpec((shape[0] // count,) + shape[1:], lambda p: (index,) + zeros)
        return pl.BlockSpec(shape[:-1] + (shape[-1] // count,), lambda p: zeros + (index,))

    specs = [spec(kind) for kind in kinds]
    return pl.pallas_call(
        whole,
        out_shape=out_shape,
        grid=(1,),
        in_specs=specs[:inputs] + anywhere(len(into) + len(behind)),
        out_specs=tuple(specs[inputs:]) if many else specs[-1],
        input_output_aliases={inputs + n: n for n in range(len(into))},
        cost_estimate=cost(us),
        compiler_params=pltpu.CompilerParams(vmem_limit_bytes=VMEM),
    )(*operands, *into, *behind)


def after(value, *others):
    return pl.pallas_call(
        lambda *refs: None,
        out_shape=jax.ShapeDtypeStruct(value.shape, value.dtype),
        in_specs=anywhere(1 + len(others)),
        out_specs=anywhere(1)[0],
        input_output_aliases={0: 0},
        cost_estimate=cost(0.1),
        compiler_params=pltpu.CompilerParams(vmem_limit_bytes=1024 * 1024),
    )(value, *others)


def held(*values):
    return pl.pallas_call(
        lambda *refs: None,
        out_shape=tuple(jax.ShapeDtypeStruct(value.shape, value.dtype) for value in values),
        in_specs=anywhere(len(values)),
        out_specs=tuple(anywhere(len(values))),
        input_output_aliases={n: n for n in range(len(values))},
        cost_estimate=cost(0.1),
        compiler_params=pltpu.CompilerParams(vmem_limit_bytes=1024 * 1024),
    )(*values)


def pole_row(lat):
    return jnp.where(lat == 0, 0, BR - 1)


def edges_kernel(cap_blocks_ref, k_ref, v_ref, cap_ref, east_ref, west_ref, sems):
    row = pole_row(lax.axis_index("lat"))
    column = pl.multiple_of(cap_blocks_ref[lax.axis_index("lon")] * BC, BC)
    copies = []
    for n, ref in enumerate((k_ref, v_ref)):
        pairs = (
            (ref.at[row, pl.ds(column, BC), :], cap_ref.at[0, n]),
            (ref.at[:, pl.ds(NB * BC - RIM, RIM), :], east_ref.at[n]),
            (ref.at[:, pl.ds(0, RIM), :], west_ref.at[n]),
        )
        for m, (source, target) in enumerate(pairs):
            copies.append(pltpu.make_async_copy(source, target, sems.at[3 * n + m]))
    for copy in copies:
        copy.start()
    for copy in copies:
        copy.wait()


def block_of(ref, prefix, column):
    return ref[prefix + (slice(None), pl.ds(column, BC), slice(None))].reshape(TOK, PAIR)


def masked_heads(block):
    lane = lax.broadcasted_iota(jnp.int32, block.shape, 1)
    zero = jnp.zeros_like(block)
    return jnp.concatenate(
        [jnp.where(lane < HSIZE, block, zero), jnp.where(lane < HSIZE, zero, block)], axis=0
    )


def query_rows(q_ref, i):
    return masked_heads(block_of(q_ref, (), i * BC) * jnp.asarray(SCALE, BF16))


def grad_rows(d_ref, i):
    return masked_heads(block_of(d_ref, (), i * BC))


def own_rows(ref):
    return jnp.concatenate([block_of(ref, (), j * BC) for j in range(NB)], axis=0)


def rim_rows(sides, n, i):
    return jnp.concatenate(
        [block_of(sides[side], (n,), block * BC) for side, block, _ in RIMS[i]], axis=0
    )


def cap_rows(cap_ref, n):
    return cap_ref[:, n].reshape(CAPK, PAIR)


def far(width, distance):
    return jnp.where(distance <= width, 0.0, FAR).astype(F32)


def cap_bias():
    lat = lax.axis_index("lat")
    return jnp.where((lat == 0) | (lat == BANDS - 1), 0.0, FAR).astype(F32)


def pieces(value):
    return [value[n * TOK : (n + 1) * TOK] for n in range(value.shape[0] // TOK)]


def column_top(scores, biases):
    tops = [s.max(0, keepdims=True) + b for s, b in zip(scores, biases)]
    top = tops[0]
    for other in tops[1:]:
        top = jnp.maximum(top, other)
    return top


def merged(scores, grads, biases, stats=None):
    top = column_top(scores, biases)
    if stats is not None:
        top = jnp.maximum(top, stats[0])
    weights = [jnp.exp(s - (top - b)) for s, b in zip(scores, biases)]
    total = sum(w.sum(0, keepdims=True) for w in weights)
    dot = sum((w * g).sum(0, keepdims=True) for w, g in zip(weights, grads))
    if stats is not None:
        fade = jnp.exp(stats[0] - top)
        total, dot = total + stats[1] * fade, dot + stats[2] * fade
    return weights, (top, total, dot)


def read_stats(ref, i):
    return tuple(ref[0, 3 * i + n : 3 * i + n + 1, :] for n in range(3))


def write_stats(ref, i, stats):
    for n, value in enumerate(stats):
        ref[0, 3 * i + n : 3 * i + n + 1, :] = value


def slopes_of(keys, values, query, grad, biases, stats):
    top, inverse, dot = stats
    weights, slopes = [], []
    for s, g, b in zip(pieces(nt(keys, query)), pieces(nt(values, grad)), biases):
        weight = jnp.exp(s - (top - b)) * inverse
        slopes.append((weight * (g - dot)).astype(BF16))
        weights.append(weight.astype(BF16))
    return jnp.concatenate(weights, axis=0), jnp.concatenate(slopes, axis=0)


def own_stats_kernel(width_ref, q_ref, k_ref, v_ref, d_ref, stats_ref):
    width = width_ref[lax.axis_index("lat")]
    keys, values = own_rows(k_ref), own_rows(v_ref)
    for i in range(NB):
        biases = [far(width, abs(j - i)) for j in range(NB)]
        scores = pieces(nt(keys, query_rows(q_ref, i)))
        grads = pieces(nt(values, grad_rows(d_ref, i)))
        write_stats(stats_ref, i, merged(scores, grads, biases)[1])


def rim_stats_kernel(width_ref, q_ref, d_ref, west_ref, east_ref, old_ref, stats_ref):
    width = width_ref[lax.axis_index("lat")]
    sides = (west_ref, east_ref)
    for i in range(NB):
        biases = [far(width, distance) for _, _, distance in RIMS[i]]
        scores = pieces(nt(rim_rows(sides, 0, i), query_rows(q_ref, i)))
        grads = pieces(nt(rim_rows(sides, 1, i), grad_rows(d_ref, i)))
        write_stats(stats_ref, i, merged(scores, grads, biases, read_stats(old_ref, i))[1])


def cap_grads_kernel(q_ref, d_ref, cap_ref, old_ref, stats_ref, keep_ref, send_ref):
    keys, values = cap_rows(cap_ref, 0), cap_rows(cap_ref, 1)
    bias = cap_bias()
    queries = [query_rows(q_ref, i) for i in range(NB)]
    outs = [grad_rows(d_ref, i) for i in range(NB)]
    weights, slopes = [], []
    for i in range(NB):
        scores, grads = nt(keys, queries[i]), nt(values, outs[i])
        (weight,), (top, total, dot) = merged([scores], [grads], [bias], read_stats(old_ref, i))
        inverse = 1.0 / total
        dot = dot * inverse
        write_stats(stats_ref, i, (top, inverse, dot))
        weight = weight * inverse
        slopes.append((weight * (grads - dot)).astype(BF16))
        weights.append(weight.astype(BF16))
    pairs = ((slopes, queries), (weights, outs))
    for n, (lefts, rights) in enumerate(pairs):
        value = nn(jnp.concatenate(lefts, axis=1), jnp.concatenate(rights, axis=0))
        value = value.reshape(LON, BC, PAIR)
        keep_ref[:, n] = value[: LON // 2]
        send_ref[:, n] = value[LON // 2 :].astype(BF16)


def heads_of(value):
    return jnp.concatenate([value[:HSIZE, :TOK], value[HSIZE:, TOK:]], axis=0)


def rim_grads_kernel(
    width_ref, q_ref, d_ref, west_ref, east_ref, stats_ref, to_west_ref, to_east_ref, ot_ref, qt_ref
):
    width = width_ref[lax.axis_index("lat")]
    sides, outs = (west_ref, east_ref), (to_west_ref, to_east_ref)
    sums = {}
    for i in range(NB):
        biases = [far(width, distance) for _, _, distance in RIMS[i]]
        query, grad = query_rows(q_ref, i), grad_rows(d_ref, i)
        keys, values = rim_rows(sides, 0, i), rim_rows(sides, 1, i)
        weights, slopes = slopes_of(keys, values, query, grad, biases, read_stats(stats_ref, i))
        ot_ref[0, i] = heads_of(nn(values.T, weights))
        qt_ref[0, i] = heads_of(nn(keys.T, slopes))
        for n, value in enumerate((nn(slopes, query), nn(weights, grad))):
            for piece, (side, block, _) in zip(pieces(value), RIMS[i]):
                key = (n, side, block)
                sums[key] = sums[key] + piece if key in sums else piece
    for (n, side, block), value in sums.items():
        outs[side][n, :, block * BC : (block + 1) * BC, :] = value.astype(BF16).reshape(
            BR, BC, PAIR
        )


def own_grads_kernel(
    width_ref,
    q_ref,
    k_ref,
    v_ref,
    d_ref,
    cap_ref,
    stats_ref,
    ot_ref,
    qt_ref,
    o_ref,
    dq_ref,
    own_ref,
):
    width = width_ref[lax.axis_index("lat")]
    bias = cap_bias()
    keys = jnp.concatenate([own_rows(k_ref), cap_rows(cap_ref, 0)], axis=0)
    values = jnp.concatenate([own_rows(v_ref), cap_rows(cap_ref, 1)], axis=0)
    keys_turned, values_turned = keys.T, values.T
    count = NB * TOK
    sums = [None, None]
    for i in range(NB):
        biases = [far(width, abs(j - i)) for j in range(NB)] + [bias] * (CAPK // TOK)
        query, grad = query_rows(q_ref, i), grad_rows(d_ref, i)
        weights, slopes = slopes_of(keys, values, query, grad, biases, read_stats(stats_ref, i))
        out = ot_ref[0, i] + heads_of(nn(values_turned, weights))
        turn = (qt_ref[0, i] + heads_of(nn(keys_turned, slopes))) * SCALE
        for ref, value in ((o_ref, out), (dq_ref, turn)):
            ref[:, i * BC : (i + 1) * BC, :] = value.T.astype(BF16).reshape(BR, BC, PAIR)
        for n, value in enumerate((nn(slopes[:count], query), nn(weights[:count], grad))):
            sums[n] = value if sums[n] is None else sums[n] + value
    for n, value in enumerate(sums):
        for j, piece in enumerate(pieces(value)):
            own_ref[n, :, j * BC : (j + 1) * BC, :] = piece.reshape(BR, BC, PAIR)


def join_kernel(
    cap_blocks_ref, own_ref, west_ref, east_ref, keep_ref, *refs
):
    row = pole_row(lax.axis_index("lat"))
    column = pl.multiple_of(cap_blocks_ref[lax.axis_index("lon")] * BC, BC)
    caps, (dk_ref, dv_ref, total) = refs[:-3], refs[-3:]
    for n, ref in enumerate((dk_ref, dv_ref)):
        total[...] = own_ref[n]
        total[:, :RIM, :] += west_ref[n].astype(F32)
        total[:, NB * BC - RIM :, :] += east_ref[n].astype(F32)
        total[row, pl.ds(column, BC), :] += keep_ref[0, n] + sum(
            ref[0, n].astype(F32) for ref in caps
        )
        ref[...] = total[...].astype(BF16)


def shards(query, keys, values, grad_out, band_width, cap_blocks):
    grid = jax.ShapeDtypeStruct(GRID, BF16)
    rim = jax.ShapeDtypeStruct(RIM_SHAPE, BF16)
    keys, values = held(keys, values)
    query, grad_out = held(query, grad_out)
    cap, to_east, to_west = pl.pallas_call(
        edges_kernel,
        out_shape=(jax.ShapeDtypeStruct((1, 2, BC, HD), BF16), rim, rim),
        in_specs=[smem()] + anywhere(2),
        out_specs=tuple(anywhere(3)),
        scratch_shapes=[pltpu.SemaphoreType.DMA((6,))],
        cost_estimate=cost(1),
        compiler_params=pltpu.CompilerParams(vmem_limit_bytes=1024 * 1024),
    )(cap_blocks, keys, values)
    west = shift(to_east, 1)
    east = shift(to_west, -1)

    g, r, w = lane_blocks(GRID), lane_blocks(RIM_SHAPE), lane_blocks((2,) + GRID)
    c, h = lane_blocks(CAP_SHAPE), lane_blocks(HALF_SHAPE)
    s, t = stat_blocks(), turn_blocks()
    received = swap(cap, YMASK)
    stats = call(
        own_stats_kernel, 0.5, [smem(), g, g, g, g], s, STATS,
        (band_width, query, keys, values, grad_out), behind=(received,),
    )
    cap = jnp.concatenate([cap, received], axis=0)
    cap = jnp.concatenate([cap] + [swap(cap, mask) for mask in XMASKS], axis=0)
    stats = call(
        rim_stats_kernel, 0.5, [smem(), g, g, r, r, s], s, STATS,
        (band_width, query, grad_out, west, east, stats),
    )
    cap = after(cap, stats)
    cap = jnp.concatenate([cap, swap(cap, CMASK)], axis=0)
    stats, keep, send = call(
        cap_grads_kernel, 3, [g, g, c, s], (s, h, h),
        (STATS, jax.ShapeDtypeStruct(HALF_SHAPE, F32), jax.ShapeDtypeStruct(HALF_SHAPE, BF16)),
        (query, grad_out, cap, stats),
    )
    def rim_part(part, into, behind):
        return call(
            rim_grads_kernel, 2.2, [smem(), g, g, r, r, s], (r, r, t, t), (rim, rim, TURNS, TURNS),
            (band_width, query, grad_out, west, east, stats), part, into, behind,
        )

    first = rim_part((0, 2), (), ())
    total = keep + swap(send, CMASK).astype(F32)
    total = total.reshape((4, 2) + total.shape[1:])
    keep, send = total[:, 0], after(total[:, 1].astype(BF16), first[0])
    received = swap(send, YMASK)
    to_west, to_east, out_turned, query_turned = rim_part((1, 2), first, (keep,))
    from_east = shift(to_west, -1)
    from_west = shift(to_east, 1)

    own_out = (grid, grid, jax.ShapeDtypeStruct((2,) + GRID, F32))
    own_in = (band_width, query, keys, values, grad_out, cap, stats, out_turned, query_turned)

    attended, query_grad, own = call(
        own_grads_kernel, 8, [smem(), g, g, g, g, c, s, t, t], (g, g, w), own_out, own_in,
        behind=(received,),
    )
    total = keep + received.astype(F32)
    keep = total[:1]
    sends = total[1:].astype(BF16)
    caps = [swap(sends[n : n + 1], mask) for n, mask in enumerate(XMASKS)]
    v = pl.BlockSpec(memory_space=pltpu.VMEM)
    key_grad, value_grad = pl.pallas_call(
        join_kernel,
        out_shape=(grid, grid),
        in_specs=[smem()] + [v] * (4 + len(caps)),
        out_specs=(v, v),
        scratch_shapes=[pltpu.VMEM(GRID, F32)],
        cost_estimate=cost(2),
        compiler_params=pltpu.CompilerParams(vmem_limit_bytes=VMEM),
    )(cap_blocks, own, from_west, from_east, keep, *caps)
    return attended, query_grad, key_grad, value_grad


def solution(mesh):
    grid = P(("dp", "lat"), "lon", None)
    return jax.shard_map(
        shards,
        mesh=mesh,
        in_specs=(grid, grid, grid, grid, P(), P()),
        out_specs=(grid, grid, grid, grid),
        check_vma=False,
    )
```

```python
import jax
import jax.numpy as jnp
from jax import lax
from jax.experimental import pallas as pl
from jax.experimental.pallas import tpu as pltpu
from jax.sharding import PartitionSpec as P

HSIZE = 64
BR = 8
BC = 16
NB = 3
HALO = 2
BANDS = 8
HD = 512
PAIR = 2 * HSIZE
PAIRS = HD // PAIR
TOK = BR * BC
ROWS2 = 2 * TOK
LON = 16
CAPK = LON * BC
RIM = HALO * BC
FAR = -1e30
SCALE = HSIZE**-0.5
XMASKS, YMASK, CMASK = (2, 4, 6), 8, 1
VMEM = 32 * 1024 * 1024
F32 = jnp.float32
BF16 = jnp.bfloat16
RIMS = (((0, 0, 2), (0, 1, 1)), ((0, 1, 2), (1, 0, 2)), ((1, 0, 1), (1, 1, 2)))


def swap(value, mask):
    return lax.ppermute(value, "lon", [(i, i ^ mask) for i in range(LON)])


def shift(value, steps):
    return lax.ppermute(value, "lon", [(i, (i + steps) % LON) for i in range(LON)])


def nt(left, right):
    return lax.dot_general(left, right, (((1,), (1,)), ((), ())), preferred_element_type=F32)


def nn(left, right):
    return lax.dot_general(left, right, (((1,), (0,)), ((), ())), preferred_element_type=F32)


def anywhere(count):
    return [pl.BlockSpec(memory_space=pl.ANY)] * count


def smem():
    return pl.BlockSpec(memory_space=pltpu.SMEM)


def cost(microseconds):
    return pl.CostEstimate(
        flops=0, bytes_accessed=int(microseconds * 3.5e6), transcendentals=0
    )


def lane_blocks(shape):
    return ("lanes", shape)


def stat_blocks():
    return ("lead", (PAIRS, 16, ROWS2))


def turn_blocks():
    return ("lead", (PAIRS, NB, PAIR, TOK))


STATS = jax.ShapeDtypeStruct((PAIRS, 16, ROWS2), F32)
TURNS = jax.ShapeDtypeStruct((PAIRS, NB, PAIR, TOK), F32)
GRID = (BR, NB * BC, HD)
RIM_SHAPE = (2, BR, RIM, HD)
CAP_SHAPE = (LON, 2, BC, HD)
HALF_SHAPE = (LON // 2, 2, BC, HD)


def call(kernel, us, ins, outs, out_shape, operands, part=(0, 1), into=(), behind=()):
    index, count = part
    many = isinstance(out_shape, tuple)
    kinds = list(ins) + (list(outs) if many else [outs])
    inputs = len(ins)

    def view(kind, ref, pair):
        if not isinstance(kind, tuple):
            return ref
        name, shape = kind
        if name == "lead":
            return ref.at[pl.ds(pair, 1)]
        return ref.at[(slice(None),) * (len(shape) - 1) + (pl.ds(pair * PAIR, PAIR),)]

    def whole(*refs):
        refs = refs[:inputs] + refs[inputs + len(into) + len(behind) :]
        for pair in range(PAIRS // count):
            kernel(*[view(kind, ref, pair) for kind, ref in zip(kinds, refs)])

    def spec(kind):
        if not isinstance(kind, tuple):
            return kind
        name, shape = kind
        zeros = (0,) * (len(shape) - 1)
        if name == "lead":
            return pl.BlockSpec((shape[0] // count,) + shape[1:], lambda p: (index,) + zeros)
        return pl.BlockSpec(shape[:-1] + (shape[-1] // count,), lambda p: zeros + (index,))

    specs = [spec(kind) for kind in kinds]
    return pl.pallas_call(
        whole,
        out_shape=out_shape,
        grid=(1,),
        in_specs=specs[:inputs] + anywhere(len(into) + len(behind)),
        out_specs=tuple(specs[inputs:]) if many else specs[-1],
        input_output_aliases={inputs + n: n for n in range(len(into))},
        cost_estimate=cost(us),
        compiler_params=pltpu.CompilerParams(vmem_limit_bytes=VMEM),
    )(*operands, *into, *behind)


def after(value, *others):
    return pl.pallas_call(
        lambda *refs: None,
        out_shape=jax.ShapeDtypeStruct(value.shape, value.dtype),
        in_specs=anywhere(1 + len(others)),
        out_specs=anywhere(1)[0],
        input_output_aliases={0: 0},
        cost_estimate=cost(0.1),
        compiler_params=pltpu.CompilerParams(vmem_limit_bytes=1024 * 1024),
    )(value, *others)


def held(*values):
    return pl.pallas_call(
        lambda *refs: None,
        out_shape=tuple(jax.ShapeDtypeStruct(value.shape, value.dtype) for value in values),
        in_specs=anywhere(len(values)),
        out_specs=tuple(anywhere(len(values))),
        input_output_aliases={n: n for n in range(len(values))},
        cost_estimate=cost(0.1),
        compiler_params=pltpu.CompilerParams(vmem_limit_bytes=1024 * 1024),
    )(*values)


def pole_row(lat):
    return jnp.where(lat == 0, 0, BR - 1)


def edges_kernel(cap_blocks_ref, k_ref, v_ref, cap_ref, east_ref, west_ref, sems):
    row = pole_row(lax.axis_index("lat"))
    column = pl.multiple_of(cap_blocks_ref[lax.axis_index("lon")] * BC, BC)
    copies = []
    for n, ref in enumerate((k_ref, v_ref)):
        pairs = (
            (ref.at[row, pl.ds(column, BC), :], cap_ref.at[0, n]),
            (ref.at[:, pl.ds(NB * BC - RIM, RIM), :], east_ref.at[n]),
            (ref.at[:, pl.ds(0, RIM), :], west_ref.at[n]),
        )
        for m, (source, target) in enumerate(pairs):
            copies.append(pltpu.make_async_copy(source, target, sems.at[3 * n + m]))
    for copy in copies:
        copy.start()
    for copy in copies:
        copy.wait()


def block_of(ref, prefix, column):
    return ref[prefix + (slice(None), pl.ds(column, BC), slice(None))].reshape(TOK, PAIR)


def masked_heads(block):
    lane = lax.broadcasted_iota(jnp.int32, block.shape, 1)
    zero = jnp.zeros_like(block)
    return jnp.concatenate(
        [jnp.where(lane < HSIZE, block, zero), jnp.where(lane < HSIZE, zero, block)], axis=0
    )


def query_rows(q_ref, i):
    return masked_heads(block_of(q_ref, (), i * BC) * jnp.asarray(SCALE, BF16))


def grad_rows(d_ref, i):
    return masked_heads(block_of(d_ref, (), i * BC))


def own_rows(ref):
    return jnp.concatenate([block_of(ref, (), j * BC) for j in range(NB)], axis=0)


def rim_rows(sides, n, i):
    return jnp.concatenate(
        [block_of(sides[side], (n,), block * BC) for side, block, _ in RIMS[i]], axis=0
    )


def cap_rows(cap_ref, n):
    return cap_ref[:, n].reshape(CAPK, PAIR)


def far(width, distance):
    return jnp.where(distance <= width, 0.0, FAR).astype(F32)


def cap_bias():
    lat = lax.axis_index("lat")
    return jnp.where((lat == 0) | (lat == BANDS - 1), 0.0, FAR).astype(F32)


def pieces(value):
    return [value[n * TOK : (n + 1) * TOK] for n in range(value.shape[0] // TOK)]


def column_top(scores, biases):
    tops = [s.max(0, keepdims=True) + b for s, b in zip(scores, biases)]
    top = tops[0]
    for other in tops[1:]:
        top = jnp.maximum(top, other)
    return top


def merged(scores, grads, biases, stats=None):
    top = column_top(scores, biases)
    if stats is not None:
        top = jnp.maximum(top, stats[0])
    weights = [jnp.exp(s - (top - b)) for s, b in zip(scores, biases)]
    total = sum(w.sum(0, keepdims=True) for w in weights)
    dot = sum((w * g).sum(0, keepdims=True) for w, g in zip(weights, grads))
    if stats is not None:
        fade = jnp.exp(stats[0] - top)
        total, dot = total + stats[1] * fade, dot + stats[2] * fade
    return weights, (top, total, dot)


def read_stats(ref, i):
    return tuple(ref[0, 3 * i + n : 3 * i + n + 1, :] for n in range(3))


def write_stats(ref, i, stats):
    for n, value in enumerate(stats):
        ref[0, 3 * i + n : 3 * i + n + 1, :] = value


def slopes_of(keys, values, query, grad, biases, stats):
    top, inverse, dot = stats
    weights, slopes = [], []
    for s, g, b in zip(pieces(nt(keys, query)), pieces(nt(values, grad)), biases):
        weight = jnp.exp(s - (top - b)) * inverse
        slopes.append((weight * (g - dot)).astype(BF16))
        weights.append(weight.astype(BF16))
    return jnp.concatenate(weights, axis=0), jnp.concatenate(slopes, axis=0)


def own_stats_kernel(width_ref, q_ref, k_ref, v_ref, d_ref, stats_ref):
    width = width_ref[lax.axis_index("lat")]
    keys, values = own_rows(k_ref), own_rows(v_ref)
    for i in range(NB):
        biases = [far(width, abs(j - i)) for j in range(NB)]
        scores = pieces(nt(keys, query_rows(q_ref, i)))
        grads = pieces(nt(values, grad_rows(d_ref, i)))
        write_stats(stats_ref, i, merged(scores, grads, biases)[1])


def rim_stats_kernel(width_ref, q_ref, d_ref, west_ref, east_ref, old_ref, stats_ref):
    width = width_ref[lax.axis_index("lat")]
    sides = (west_ref, east_ref)
    for i in range(NB):
        biases = [far(width, distance) for _, _, distance in RIMS[i]]
        scores = pieces(nt(rim_rows(sides, 0, i), query_rows(q_ref, i)))
        grads = pieces(nt(rim_rows(sides, 1, i), grad_rows(d_ref, i)))
        write_stats(stats_ref, i, merged(scores, grads, biases, read_stats(old_ref, i))[1])


def cap_grads_kernel(q_ref, d_ref, cap_ref, old_ref, stats_ref, keep_ref, send_ref):
    keys, values = cap_rows(cap_ref, 0), cap_rows(cap_ref, 1)
    bias = cap_bias()
    queries = [query_rows(q_ref, i) for i in range(NB)]
    outs = [grad_rows(d_ref, i) for i in range(NB)]
    weights, slopes = [], []
    for i in range(NB):
        scores, grads = nt(keys, queries[i]), nt(values, outs[i])
        (weight,), (top, total, dot) = merged([scores], [grads], [bias], read_stats(old_ref, i))
        inverse = 1.0 / total
        dot = dot * inverse
        write_stats(stats_ref, i, (top, inverse, dot))
        weight = weight * inverse
        slopes.append((weight * (grads - dot)).astype(BF16))
        weights.append(weight.astype(BF16))
    pairs = ((slopes, queries), (weights, outs))
    for n, (lefts, rights) in enumerate(pairs):
        value = nn(jnp.concatenate(lefts, axis=1), jnp.concatenate(rights, axis=0))
        value = value.reshape(LON, BC, PAIR)
        keep_ref[:, n] = value[: LON // 2]
        send_ref[:, n] = value[LON // 2 :].astype(BF16)


def heads_of(value):
    return jnp.concatenate([value[:HSIZE, :TOK], value[HSIZE:, TOK:]], axis=0)


def rim_grads_kernel(
    width_ref, q_ref, d_ref, west_ref, east_ref, stats_ref, to_west_ref, to_east_ref, ot_ref, qt_ref
):
    width = width_ref[lax.axis_index("lat")]
    sides, outs = (west_ref, east_ref), (to_west_ref, to_east_ref)
    sums = {}
    for i in range(NB):
        biases = [far(width, distance) for _, _, distance in RIMS[i]]
        query, grad = query_rows(q_ref, i), grad_rows(d_ref, i)
        keys, values = rim_rows(sides, 0, i), rim_rows(sides, 1, i)
        weights, slopes = slopes_of(keys, values, query, grad, biases, read_stats(stats_ref, i))
        ot_ref[0, i] = heads_of(nn(values.T, weights))
        qt_ref[0, i] = heads_of(nn(keys.T, slopes))
        for n, value in enumerate((nn(slopes, query), nn(weights, grad))):
            for piece, (side, block, _) in zip(pieces(value), RIMS[i]):
                key = (n, side, block)
                sums[key] = sums[key] + piece if key in sums else piece
    for (n, side, block), value in sums.items():
        outs[side][n, :, block * BC : (block + 1) * BC, :] = value.astype(BF16).reshape(
            BR, BC, PAIR
        )


def own_grads_kernel(
    width_ref,
    q_ref,
    k_ref,
    v_ref,
    d_ref,
    cap_ref,
    stats_ref,
    ot_ref,
    qt_ref,
    o_ref,
    dq_ref,
    own_ref,
):
    width = width_ref[lax.axis_index("lat")]
    bias = cap_bias()
    keys = jnp.concatenate([own_rows(k_ref), cap_rows(cap_ref, 0)], axis=0)
    values = jnp.concatenate([own_rows(v_ref), cap_rows(cap_ref, 1)], axis=0)
    keys_turned, values_turned = keys.T, values.T
    count = NB * TOK
    sums = [None, None]
    for i in range(NB):
        biases = [far(width, abs(j - i)) for j in range(NB)] + [bias] * (CAPK // TOK)
        query, grad = query_rows(q_ref, i), grad_rows(d_ref, i)
        weights, slopes = slopes_of(keys, values, query, grad, biases, read_stats(stats_ref, i))
        out = ot_ref[0, i] + heads_of(nn(values_turned, weights))
        turn = (qt_ref[0, i] + heads_of(nn(keys_turned, slopes))) * SCALE
        for ref, value in ((o_ref, out), (dq_ref, turn)):
            ref[:, i * BC : (i + 1) * BC, :] = value.T.astype(BF16).reshape(BR, BC, PAIR)
        for n, value in enumerate((nn(slopes[:count], query), nn(weights[:count], grad))):
            sums[n] = value if sums[n] is None else sums[n] + value
    for n, value in enumerate(sums):
        for j, piece in enumerate(pieces(value)):
            own_ref[n, :, j * BC : (j + 1) * BC, :] = piece.reshape(BR, BC, PAIR)


def join_kernel(
    cap_blocks_ref, own_ref, west_ref, east_ref, keep_ref, *refs
):
    row = pole_row(lax.axis_index("lat"))
    column = pl.multiple_of(cap_blocks_ref[lax.axis_index("lon")] * BC, BC)
    caps, (dk_ref, dv_ref, total) = refs[:-3], refs[-3:]
    for n, ref in enumerate((dk_ref, dv_ref)):
        total[...] = own_ref[n]
        total[:, :RIM, :] += west_ref[n].astype(F32)
        total[:, NB * BC - RIM :, :] += east_ref[n].astype(F32)
        total[row, pl.ds(column, BC), :] += keep_ref[0, n] + sum(
            ref[0, n].astype(F32) for ref in caps
        )
        ref[...] = total[...].astype(BF16)


def shards(query, keys, values, grad_out, band_width, cap_blocks):
    grid = jax.ShapeDtypeStruct(GRID, BF16)
    rim = jax.ShapeDtypeStruct(RIM_SHAPE, BF16)
    keys, values = held(keys, values)
    query, grad_out = held(query, grad_out)
    cap, to_east, to_west = pl.pallas_call(
        edges_kernel,
        out_shape=(jax.ShapeDtypeStruct((1, 2, BC, HD), BF16), rim, rim),
        in_specs=[smem()] + anywhere(2),
        out_specs=tuple(anywhere(3)),
        scratch_shapes=[pltpu.SemaphoreType.DMA((6,))],
        cost_estimate=cost(1),
        compiler_params=pltpu.CompilerParams(vmem_limit_bytes=1024 * 1024),
    )(cap_blocks, keys, values)
    west = shift(to_east, 1)
    east = shift(to_west, -1)

    g, r, w = lane_blocks(GRID), lane_blocks(RIM_SHAPE), lane_blocks((2,) + GRID)
    c, h = lane_blocks(CAP_SHAPE), lane_blocks(HALF_SHAPE)
    s, t = stat_blocks(), turn_blocks()
    received = swap(cap, YMASK)
    stats = call(
        own_stats_kernel, 0.5, [smem(), g, g, g, g], s, STATS,
        (band_width, query, keys, values, grad_out), behind=(received,),
    )
    cap = jnp.concatenate([cap, received], axis=0)
    cap = jnp.concatenate([cap] + [swap(cap, mask) for mask in XMASKS], axis=0)
    stats = call(
        rim_stats_kernel, 0.5, [smem(), g, g, r, r, s], s, STATS,
        (band_width, query, grad_out, west, east, stats),
    )
    cap = after(cap, stats)
    cap = jnp.concatenate([cap, swap(cap, CMASK)], axis=0)
    stats, keep, send = call(
        cap_grads_kernel, 3, [g, g, c, s], (s, h, h),
        (STATS, jax.ShapeDtypeStruct(HALF_SHAPE, F32), jax.ShapeDtypeStruct(HALF_SHAPE, BF16)),
        (query, grad_out, cap, stats),
    )
    def rim_part(part, into, behind):
        return call(
            rim_grads_kernel, 2.2, [smem(), g, g, r, r, s], (r, r, t, t), (rim, rim, TURNS, TURNS),
            (band_width, query, grad_out, west, east, stats), part, into, behind,
        )

    first = rim_part((0, 2), (), ())
    total = keep + swap(send, CMASK).astype(F32)
    total = total.reshape((4, 2) + total.shape[1:])
    keep, send = total[:, 0], after(total[:, 1].astype(BF16), first[0])
    received = swap(send, YMASK)
    to_west, to_east, out_turned, query_turned = rim_part((1, 2), first, (keep,))
    from_east = shift(to_west, -1)
    from_west = shift(to_east, 1)

    own_out = (grid, grid, jax.ShapeDtypeStruct((2,) + GRID, F32))
    own_in = (band_width, query, keys, values, grad_out, cap, stats, out_turned, query_turned)

    def own_part(part, into):
        kinds = [smem(), g, g, g, g, c, s, t, t]
        return call(own_grads_kernel, 4, kinds, (g, g, w), own_out, own_in, part, into, (received,))

    first = own_part((0, 2), ())
    total = keep + received.astype(F32)
    keep = total[:1]
    sends = after(total[1:].astype(BF16), first[2])
    caps = [swap(sends[n : n + 1], mask) for n, mask in enumerate(XMASKS)]
    attended, query_grad, own = own_part((1, 2), first)
    v = pl.BlockSpec(memory_space=pltpu.VMEM)
    key_grad, value_grad = pl.pallas_call(
        join_kernel,
        out_shape=(grid, grid),
        in_specs=[smem()] + [v] * (4 + len(caps)),
        out_specs=(v, v),
        scratch_shapes=[pltpu.VMEM(GRID, F32)],
        cost_estimate=cost(2),
        compiler_params=pltpu.CompilerParams(vmem_limit_bytes=VMEM),
    )(cap_blocks, own, from_west, from_east, keep, *caps)
    return attended, query_grad, key_grad, value_grad


def solution(mesh):
    grid = P(("dp", "lat"), "lon", None)
    return jax.shard_map(
        shards,
        mesh=mesh,
        in_specs=(grid, grid, grid, grid, P(), P()),
        out_specs=(grid, grid, grid, grid),
        check_vma=False,
    )
```
